768 devices in a mesh: blk: 64 (over y, x, core), sig: 12 (over z).
Axes of the slice: x: 4, y: 8, z: 12, core: 2. Of those that a mesh axis runs over, the one named last changes fastest.
Arguments:
- coarse_fields: float32 [98304, 3, 512], P(('blk', 'sig')), may hold values from -6 to 6
- fine_fields: float32 [24576, 3, 8, 512], P(('blk', 'sig')), may hold values from -6 to 6
- owner: int32 [24576, 1], P(('blk', 'sig')), may hold values from 0 to 63, as said below
- target_tile: int32 [24576, 1], P(('blk', 'sig')), may hold values from 0 to 127, as said below
- tags: int32 [98304, 512], P(('blk', 'sig')), may hold values 0 or 1
Outputs:
- synced: float32 [98304, 3, 512], P(('blk', 'sig'))
- signature: float32 [64, 1032], P('blk')
The draws below stay inside these ranges and needn't reach their ends.
Inputs may be any that keep to these rules, and one draw needn't show every extreme that they name: On the 32 patches of one device at most 2 name the same owner; in every sig slab some devices name one owner exactly 2 times. `target_tile`: among the patches of all devices with one sig index no owner and tile is named twice; in every sig slab one owner has all 128 of its tiles named.
All inputs are finite; a program needn't handle non-finite values. No bound on the sum of `tags` on one device may be relied on, other than what follows from the above.
Results may differ from the reference program's by a relative error of at most 0.0002.
Values sent between devices are 32-bit elements; how exact they have to be, the bound alone decides.
No kernel may reach another device: no remote copies, remote signals or barrier semaphores. Data moves between devices by JAX's collectives and lax.ppermute only.
A program may use at most 32 MiB of HBM per device.

```python
import jax
import jax.numpy as jnp

EDGE = 8
CELLS = 512
TILES_DEV = 128
PATCH_DEV = 32
CAP = 2
TILES = 98304
PATCHES = 24576
N_BLK = 64
N_SIG = 12


def plan_patches(key):
    base = jax.random.fold_in(key, 4111)
    streams = jax.random.split(base, 5)
    heavy = jax.random.randint(streams[0], (N_SIG, 1, 1), 0, N_BLK).astype(jnp.int32)
    source_ids = jnp.arange(N_BLK, dtype=jnp.int32)[None, :]
    rank_scores = jax.random.randint(streams[1], (N_SIG, N_BLK), 0, 65536).astype(jnp.int32) * N_BLK + source_ids
    sources_sorted = jnp.argsort(rank_scores, axis=1)
    source_rank = jnp.argsort(sources_sorted, axis=1).astype(jnp.int32)
    heavy_share = jnp.clip(TILES_DEV - CAP * source_rank, 0, CAP)[:, :, None]
    offset = jax.random.randint(streams[2], (N_SIG, N_BLK, 1), 0, N_BLK - 1).astype(jnp.int32)
    position = jnp.arange(PATCH_DEV, dtype=jnp.int32)[None, None, :]
    spread = (offset + position - heavy_share) % (N_BLK - 1)
    logical = jnp.where(position < heavy_share, heavy, (heavy + 1 + spread) % N_BLK)
    position_scores = jax.random.randint(streams[3], (N_SIG, N_BLK, PATCH_DEV), 0, 65536).astype(jnp.int32) * PATCH_DEV + position
    shuffle = jnp.argsort(position_scores, axis=2)
    owners = jnp.take_along_axis(logical, shuffle, axis=2).astype(jnp.int32)
    flat_owner = owners.reshape(N_SIG, N_BLK * PATCH_DEV)
    matches = (flat_owner[:, :, None] == jnp.arange(N_BLK, dtype=jnp.int32)[None, None, :]).astype(jnp.int32)
    earlier = jnp.cumsum(matches, axis=1) - matches
    arrival = jnp.sum(earlier * matches, axis=2).astype(jnp.int32)
    tile_ids = jnp.arange(TILES_DEV, dtype=jnp.int32)[None, None, :]
    tile_scores = jax.random.randint(streams[4], (N_SIG, N_BLK, TILES_DEV), 0, 65536).astype(jnp.int32) * TILES_DEV + tile_ids
    tile_order = jnp.argsort(tile_scores, axis=2).astype(jnp.int32).reshape(N_SIG, N_BLK * TILES_DEV)
    target = jnp.take_along_axis(tile_order, flat_owner * TILES_DEV + arrival, axis=1).astype(jnp.int32)
    owner_out = jnp.transpose(owners, (1, 0, 2)).reshape(PATCHES, 1)
    target_out = jnp.transpose(target.reshape(N_SIG, N_BLK, PATCH_DEV), (1, 0, 2)).reshape(PATCHES, 1)
    return (owner_out.astype(jnp.int32), target_out.astype(jnp.int32))


def draw_owner(key, part):
    return plan_patches(key)[0]


def draw_target_tile(key, part):
    return plan_patches(key)[1]


def touch_ends(result, own_key, low, largest):
    place = [jax.random.randint(jax.random.fold_in(own_key, axis), (), 0, length) for axis, length in enumerate(result.shape)]
    longest = result.shape.index(max(result.shape))
    next_to = place[:longest] + [(place[longest] + 1) % result.shape[longest]] + place[longest + 1:]
    return result.at[tuple(place)].set(low).at[tuple(next_to)].set(largest)


def levels(own_key, dims, cuts, low, largest):
    def one(dim, blocks):
        steps = jax.random.uniform(jax.random.fold_in(jax.random.fold_in(own_key, 6), dim), (blocks,), jnp.float32, low / len(cuts), largest / len(cuts))
        return jnp.repeat(jnp.exp(steps), dims[dim] // blocks).reshape((-1,) + (1,) * (len(dims) - dim - 1))

    level = one(*cuts[0])
    for cut in cuts[1:]:
        level = level * one(*cut)
    return level


def scatter_about(stream_key, extent, deviation, bound, pieces=(), kind=jnp.bfloat16):
    entries = deviation * jax.random.normal(stream_key, extent, jnp.float32)
    if pieces:
        entries = entries * levels(stream_key, extent, pieces, -0.22, 0.18)
    return jnp.clip(entries, -bound, bound).astype(kind)


def setup_inputs(seed: int = 0) -> dict:
    key_list = jax.random.split(jax.random.key(seed), 6)
    return {
        "coarse_fields": scatter_about(key_list[0], (TILES, 3, CELLS), 1.0, 6.0, ((0, 768),), jnp.float32),
        "fine_fields": scatter_about(key_list[1], (PATCHES, 3, 8, CELLS), 1.0, 6.0, ((0, 768),), jnp.float32),
        "owner": draw_owner(jax.random.fold_in(key_list[5], 71), 0),
        "target_tile": draw_target_tile(jax.random.fold_in(key_list[5], 71), 0),
        "tags": touch_ends((jax.random.randint(key_list[4], (TILES, CELLS), 0, 2) < 1).astype(jnp.int32), jax.random.fold_in(key_list[4], 1), 0, 1),
    }


def indicator_of(fields):
    total = jnp.zeros(fields.shape[:1] + fields.shape[2:], jnp.float32)
    for axis_number in (2, 3, 4):
        upper = jax.lax.slice_in_dim(fields, 2, EDGE, axis=axis_number)
        lower = jax.lax.slice_in_dim(fields, 0, EDGE - 2, axis=axis_number)
        middle = 0.5 * (upper - lower)
        widths = [(0, 0)] * 5
        widths[axis_number] = (1, 1)
        padded = jnp.pad(middle, widths)
        total = total + jnp.sum(padded * padded, axis=1)
    return total


def reference(coarse_fields, fine_fields, owner, target_tile, tags):
    averaged = (0.125 * jnp.sum(fine_fields, axis=2)).reshape(PATCHES, 3 * CELLS)
    device = jnp.arange(PATCHES, dtype=jnp.int32) // PATCH_DEV
    slab = device % N_SIG
    tile_ids = ((owner[:, 0] * N_SIG + slab) * TILES_DEV + target_tile[:, 0]).astype(jnp.int32)
    totals = jax.ops.segment_sum(averaged, tile_ids, num_segments=TILES)
    covered = jax.ops.segment_sum(jnp.ones((PATCHES,), jnp.float32), tile_ids, num_segments=TILES)
    flat = coarse_fields.reshape(TILES, 3 * CELLS)
    synced = jnp.where(covered[:, None] > 0, totals, flat)
    synced = synced.reshape(TILES, 3, CELLS)
    indicator = indicator_of(synced.reshape(TILES, 3, EDGE, EDGE, EDGE))
    weight = tags.reshape(TILES, EDGE, EDGE, EDGE).astype(jnp.float32) * indicator
    weight = weight.reshape(N_BLK, N_SIG, TILES_DEV, EDGE, EDGE, EDGE)
    along_y = jnp.sum(weight, axis=(1, 3, 5)).reshape(N_BLK, TILES_DEV * EDGE) / (EDGE * EDGE * N_SIG)
    along_z = jnp.sum(weight, axis=(1, 2, 3, 4)) / (EDGE * EDGE * TILES_DEV * N_SIG)
    signature = jnp.concatenate([along_y, along_z], axis=1)
    return synced, signature
```

```python
import jax
import jax.numpy as jnp
from jax import lax
from jax.experimental import pallas as pl
from jax.experimental.pallas import tpu as pltpu
from jax.sharding import PartitionSpec as P

EDGE = 8
CAP = 2
LANES = 128
CHUNKS = 4


def pack_kernel(owner, target, fine, out, buf, count, sems):
    patches, fields, children, cells = fine.shape
    chunk = patches // CHUNKS
    per_field = cells // LANES
    block = out.shape[0] // count.shape[0]
    tag_row = CAP * fields * per_field

    def fetch(k):
        part = pl.ds(k * chunk, chunk)
        return pltpu.make_async_copy(fine.at[part], buf.at[part], sems.at[k])

    for k in range(CHUNKS):
        fetch(k).start()
    lane = lax.broadcasted_iota(jnp.int32, (1, LANES), 1)
    zero_row = jnp.zeros((1, LANES), jnp.float32)
    for o in range(count.shape[0]):
        count[o] = 0
        out[o * block + tag_row] = zero_row
    first_row = []
    for i in range(patches):
        o = owner[i]
        rank = count[o]
        count[o] = rank + 1
        row = o * block + tag_row
        mark = (target[i] + 1).astype(jnp.float32)
        out[row] = jnp.where(lane == rank, mark, out[row])
        first_row.append(o * block + rank * (fields * per_field))
    for k in range(CHUNKS):
        fetch(k).wait()
        for i in range(k * chunk, (k + 1) * chunk):
            for f in range(fields):
                mean = 0.125 * jnp.sum(buf[i, f], axis=0, keepdims=True)
                for c in range(per_field):
                    out[first_row[i] + f * per_field + c] = mean[:, c * LANES : (c + 1) * LANES]


def pack(owner, target, fine, blocks):
    patches, fields, children, cells = fine.shape
    block = CAP * fields * cells // LANES + 1
    return pl.pallas_call(
        pack_kernel,
        out_shape=jax.ShapeDtypeStruct((blocks * block, 1, LANES), jnp.float32),
        in_specs=[
            pl.BlockSpec(memory_space=pltpu.SMEM),
            pl.BlockSpec(memory_space=pltpu.SMEM),
            pl.BlockSpec(memory_space=pl.ANY),
        ],
        out_specs=pl.BlockSpec(memory_space=pltpu.VMEM),
        scratch_shapes=[
            pltpu.VMEM(fine.shape, jnp.float32),
            pltpu.SMEM((blocks,), jnp.int32),
            pltpu.SemaphoreType.DMA((CHUNKS,)),
        ],
        compiler_params=pltpu.CompilerParams(vmem_limit_bytes=16 * 2**20),
        name="pack_patches",
    )(owner, target, fine)


def tile_kernel(got, coarse, tags, synced, parts, field_buf, marks, marks_f, weight_buf, sem):
    fields, tiles, cells = coarse.shape
    per_field = cells // LANES
    slot_rows = fields * per_field
    block = CAP * slot_rows + 1
    blocks = got.shape[0] // block
    copies, part_rows = parts.shape[0], parts.shape[1]
    y_rows = part_rows - 1

    for b in range(blocks):
        marks[b] = got[b * block + CAP * slot_rows]
    to_scalar = pltpu.make_async_copy(marks, marks_f, sem)
    to_scalar.start()
    for f in range(fields):
        for c in range(per_field):
            field_buf[f * per_field + c, :tiles] = coarse[f, :, c * LANES : (c + 1) * LANES]
    to_scalar.wait()
    for b in range(blocks):
        for r in range(CAP):
            mark = marks_f[b, 0, r].astype(jnp.int32)
            tile = jnp.where(mark > 0, mark - 1, tiles)
            base = b * block + r * slot_rows
            for j in range(slot_rows):
                field_buf[j, pl.ds(tile, 1)] = got[base + j]

    lane = lax.broadcasted_iota(jnp.int32, (EDGE, LANES), 1)
    z = lane % EDGE
    y = (lane // EDGE) % EDGE
    upper = lane >= EDGE * EDGE
    inner_z = (z > 0) & (z < EDGE - 1)
    inner_y = (y > 0) & (y < EDGE - 1)
    total = jnp.zeros((EDGE, LANES), jnp.float32)
    for g in range(tiles // 8):
        rows = pl.ds(g * 8, 8)
        sum_z = [None] * per_field
        sum_y = [None] * per_field
        sum_x = [None] * (per_field - 1)
        for f in range(fields):
            v = [field_buf[f * per_field + c, rows] for c in range(per_field)]
            for c in range(per_field):
                synced[f, rows, c * LANES : (c + 1) * LANES] = v[c]
                dz = v[c] - pltpu.roll(v[c], 2, 1)
                dy = v[c] - pltpu.roll(v[c], 2 * EDGE, 1)
                sum_z[c] = dz * dz if f == 0 else sum_z[c] + dz * dz
                sum_y[c] = dy * dy if f == 0 else sum_y[c] + dy * dy
                if c:
                    dx = v[c] - v[c - 1]
                    sum_x[c - 1] = dx * dx if f == 0 else sum_x[c - 1] + dx * dx
        turned = [pltpu.roll(s, EDGE * EDGE, 1) for s in sum_x]
        weight = None
        for c in range(per_field):
            along_z = jnp.where(inner_z, pltpu.roll(sum_z[c], LANES - 1, 1), 0.0)
            along_y = jnp.where(inner_y, pltpu.roll(sum_y[c], LANES - EDGE, 1), 0.0)
            above = turned[c] if c < per_field - 1 else jnp.zeros_like(along_z)
            below = turned[c - 1] if c else jnp.zeros_like(along_z)
            along_x = jnp.where(upper, above, below)
            tag = tags[rows, c * LANES : (c + 1) * LANES].astype(jnp.float32)
            term = tag * (along_x + along_y + along_z)
            weight = term if c == 0 else weight + term
        weight_buf[rows] = weight
        total = total + weight
    weight_buf[pl.ds(tiles, 8)] = total

    src = lax.broadcasted_iota(jnp.int32, (LANES, LANES), 0)
    dst = lax.broadcasted_iota(jnp.int32, (LANES, LANES), 1)
    pick_y = ((src // EDGE) % EDGE == dst % EDGE).astype(jnp.float32)
    pick_z = (src % EDGE == dst).astype(jnp.float32)
    high = lax.Precision.HIGHEST
    by_y = jnp.dot(
        weight_buf[:tiles], pick_y, precision=high, preferred_element_type=jnp.float32
    )
    by_z = jnp.dot(
        weight_buf[pl.ds(tiles, 8)], pick_z, precision=high, preferred_element_type=jnp.float32
    )
    per_row = LANES // EDGE
    row_tile = lax.broadcasted_iota(jnp.int32, (per_row, LANES), 0)
    row_lane = lax.broadcasted_iota(jnp.int32, (per_row, LANES), 1)
    own = row_lane // EDGE == row_tile
    for r in range(y_rows):
        piece = jnp.where(own, by_y[r * per_row : (r + 1) * per_row], 0.0)
        line = 0.25 * jnp.sum(piece, axis=0, keepdims=True)
        for k in range(copies):
            parts[k, r] = line
    line = 0.25 * jnp.sum(by_z, axis=0, keepdims=True)
    for k in range(copies):
        parts[k, y_rows] = line


def tile_step(got, coarse, tags, slabs):
    fields, tiles, cells = coarse.shape
    block = CAP * fields * cells // LANES + 1
    blocks = got.shape[0] // block
    part_rows = tiles * EDGE // LANES + 1
    vmem = pl.BlockSpec(memory_space=pltpu.VMEM)
    return pl.pallas_call(
        tile_kernel,
        out_shape=(
            jax.ShapeDtypeStruct(coarse.shape, jnp.float32),
            jax.ShapeDtypeStruct((slabs, part_rows, 1, LANES), jnp.float32),
        ),
        in_specs=[vmem, vmem, vmem],
        out_specs=(vmem, vmem),
        scratch_shapes=[
            pltpu.VMEM((fields * cells // LANES, tiles + 8, LANES), jnp.float32),
            pltpu.VMEM((blocks, 1, LANES), jnp.float32),
            pltpu.SMEM((blocks, 1, LANES), jnp.float32),
            pltpu.VMEM((tiles + 8, LANES), jnp.float32),
            pltpu.SemaphoreType.DMA,
        ],
        compiler_params=pltpu.CompilerParams(vmem_limit_bytes=16 * 2**20),
        name="tile_step",
    )(got, coarse, tags)


def sum_kernel(along_y_cells, along_z_cells, parts, out):
    y_rows = parts.shape[1] - 1
    for r in range(y_rows + 1):
        line = parts[0, r]
        for k in range(1, parts.shape[0]):
            line = line + parts[k, r]
        if r < y_rows:
            out[:, r * LANES : (r + 1) * LANES] = line * (1.0 / along_y_cells)
        else:
            out[:, r * LANES :] = line[:, :EDGE] * (1.0 / along_z_cells)


def sum_parts(parts, tiles, slabs):
    width = tiles * EDGE + EDGE
    along_y_cells = EDGE * EDGE * slabs
    along_z_cells = EDGE * EDGE * tiles * slabs
    return pl.pallas_call(
        lambda p, o: sum_kernel(along_y_cells, along_z_cells, p, o),
        out_shape=jax.ShapeDtypeStruct((1, width), jnp.float32),
        in_specs=[pl.BlockSpec(memory_space=pltpu.VMEM)],
        out_specs=pl.BlockSpec(memory_space=pltpu.VMEM),
        name="sum_parts",
    )(parts)


def shards(coarse_fields, fine_fields, owner, target_tile, tags):
    tiles = coarse_fields.shape[0]
    blocks = lax.axis_size("blk")
    slabs = lax.axis_size("sig")
    sent = pack(owner[:, 0], target_tile[:, 0], fine_fields, blocks)
    rows = sent.shape[0] // blocks
    got = lax.all_to_all(
        sent.reshape(blocks, rows, 1, LANES), "blk", split_axis=0, concat_axis=0, tiled=True
    )
    got = got.reshape(blocks * rows, 1, LANES)
    coarse = jnp.transpose(coarse_fields, (1, 0, 2))
    synced, parts = tile_step(got, coarse, tags, slabs)
    parts = lax.all_to_all(parts, "sig", split_axis=0, concat_axis=0, tiled=True)
    signature = sum_parts(parts, tiles, slabs)
    return (jnp.transpose(synced, (1, 0, 2)), signature)


def solution(mesh):
    return jax.shard_map(
        shards,
        mesh=mesh,
        in_specs=(
            P(("blk", "sig"), None, None),
            P(("blk", "sig"), None, None, None),
            P(("blk", "sig"), None),
            P(("blk", "sig"), None),
            P(("blk", "sig"), None),
        ),
        out_specs=(P(("blk", "sig"), None, None), P("blk", None)),
        check_vma=False,
    )
```

```python
import jax
import jax.numpy as jnp
from jax import lax
from jax.experimental import pallas as pl
from jax.experimental.pallas import tpu as pltpu
from jax.sharding import PartitionSpec as P

EDGE = 8
CAP = 2
LANES = 128
CHUNKS = 4


def pack_kernel(owner, target, fine, out, buf, means, marks, owner_s, target_s, count, sems):
    patches, fields, children, cells = fine.shape
    chunk = patches // CHUNKS
    per_field = cells // LANES
    slot_rows = fields * per_field
    blocks = out.shape[0]

    def fetch(k):
        part = pl.ds(k * chunk, chunk)
        return pltpu.make_async_copy(fine.at[part], buf.at[part], sems.at[k])

    owner_copy = pltpu.make_async_copy(owner, owner_s, sems.at[CHUNKS])
    target_copy = pltpu.make_async_copy(target, target_s, sems.at[CHUNKS + 1])
    owner_copy.start()
    target_copy.start()
    for k in range(CHUNKS):
        fetch(k).start()
    lane = lax.broadcasted_iota(jnp.int32, (1, LANES), 1)
    own_lane = CAP * lax.axis_index("blk")
    for o in range(blocks):
        count[o] = 0
        marks[o] = jnp.zeros((1, LANES), jnp.float32)
    owner_copy.wait()
    target_copy.wait()
    slots = []
    for i in range(patches):
        o = owner_s[i]
        rank = count[o]
        count[o] = rank + 1
        mark = (target_s[i] + 1).astype(jnp.float32)
        marks[o] = jnp.where(lane == own_lane + rank, mark, marks[o])
        slots.append((o, rank))
    leave_marks = pltpu.make_async_copy(marks, out.at[:, CAP * slot_rows], sems.at[CHUNKS + 2])
    leave_marks.start()

    def leave(i):
        o, rank = slots[i]
        return pltpu.make_async_copy(
            means.at[pl.ds(i * slot_rows, slot_rows)],
            out.at[o, pl.ds(rank * slot_rows, slot_rows)],
            sems.at[CHUNKS + 3 + i],
        )

    for k in range(CHUNKS):
        fetch(k).wait()
        for i in range(k * chunk, (k + 1) * chunk):
            for f in range(fields):
                mean = 0.125 * jnp.sum(buf[i, f], axis=0, keepdims=True)
                for c in range(per_field):
                    means[i * slot_rows + f * per_field + c] = mean[:, c * LANES : (c + 1) * LANES]
            leave(i).start()
    leave_marks.wait()
    for i in range(patches):
        leave(i).wait()


def pack(owner, target, fine, blocks):
    patches, fields, children, cells = fine.shape
    slot_rows = fields * cells // LANES
    hbm = pl.BlockSpec(memory_space=pltpu.HBM)
    return pl.pallas_call(
        pack_kernel,
        out_shape=jax.ShapeDtypeStruct((blocks, CAP * slot_rows + 1, 1, LANES), jnp.float32),
        in_specs=[hbm, hbm, hbm],
        out_specs=hbm,
        scratch_shapes=[
            pltpu.VMEM(fine.shape, jnp.float32),
            pltpu.VMEM((patches * slot_rows, 1, LANES), jnp.float32),
            pltpu.VMEM((blocks, 1, LANES), jnp.float32),
            pltpu.SMEM((patches,), jnp.int32),
            pltpu.SMEM((patches,), jnp.int32),
            pltpu.SMEM((blocks,), jnp.int32),
            pltpu.SemaphoreType.DMA((CHUNKS + 3 + patches,)),
        ],
        compiler_params=pltpu.CompilerParams(vmem_limit_bytes=60 * 2**20),
        name="pack_patches",
    )(owner, target, fine)


def tile_kernel(got, coarse, tags, synced, parts, fields_v, marks_v, marks_s, weight_v, sems):
    fields, tiles, cells = coarse.shape
    per_field = cells // LANES
    slot_rows = fields * per_field
    block = CAP * slot_rows + 1
    blocks = got.shape[0] // block
    pitch = tiles + 8
    copies, part_rows = parts.shape[0], parts.shape[1]
    y_rows = part_rows - 1

    marks = [None] * 4
    for b in range(blocks):
        row = got[pl.ds(b * block + CAP * slot_rows, 1)]
        marks[b % 4] = row if b < 4 else marks[b % 4] + row
    mark = ((marks[0] + marks[1]) + (marks[2] + marks[3])).astype(jnp.int32)
    marks_v[...] = jnp.where(mark > 0, mark - 1, tiles)
    to_scalar = pltpu.make_async_copy(marks_v, marks_s, sems.at[slot_rows])
    to_scalar.start()
    for f in range(fields):
        for c in range(per_field):
            fields_v[pl.ds((f * per_field + c) * pitch, tiles)] = coarse[
                f, :, c * LANES : (c + 1) * LANES
            ]
    to_scalar.wait()
    for b in range(blocks):
        for r in range(CAP):
            tile = marks_s[0, CAP * b + r]
            base = b * block + r * slot_rows
            for j in range(0, slot_rows, 8):
                n = min(8, slot_rows - j)
                fields_v[pl.ds(tile + j * pitch, n, stride=pitch)] = got[base + j : base + j + n]

    def leave(f, c):
        j = f * per_field + c
        return pltpu.make_async_copy(
            fields_v.at[pl.ds(j * pitch, tiles)],
            synced.at[f, :, pl.ds(c * LANES, LANES)],
            sems.at[j],
        )

    for f in range(fields):
        for c in range(per_field):
            leave(f, c).start()

    lane = lax.broadcasted_iota(jnp.int32, (EDGE, LANES), 1)
    z = lane % EDGE
    y = (lane // EDGE) % EDGE
    upper = lane >= EDGE * EDGE
    inner_z = (z > 0) & (z < EDGE - 1)
    inner_y = (y > 0) & (y < EDGE - 1)
    total = jnp.zeros((EDGE, LANES), jnp.float32)
    for g in range(tiles // 8):
        rows = pl.ds(g * 8, 8)
        sum_z = [None] * per_field
        sum_y = [None] * per_field
        sum_x = [None] * (per_field - 1)
        for f in range(fields):
            v = [fields_v[pl.ds((f * per_field + c) * pitch + g * 8, 8)] for c in range(per_field)]
            for c in range(per_field):
                dz = v[c] - pltpu.roll(v[c], 2, 1)
                dy = v[c] - pltpu.roll(v[c], 2 * EDGE, 1)
                sum_z[c] = dz * dz if f == 0 else sum_z[c] + dz * dz
                sum_y[c] = dy * dy if f == 0 else sum_y[c] + dy * dy
                if c:
                    dx = v[c] - v[c - 1]
                    sum_x[c - 1] = dx * dx if f == 0 else sum_x[c - 1] + dx * dx
        turned = [pltpu.roll(s, EDGE * EDGE, 1) for s in sum_x]
        weight = None
        for c in range(per_field):
            along_z = jnp.where(inner_z, pltpu.roll(sum_z[c], LANES - 1, 1), 0.0)
            along_y = jnp.where(inner_y, pltpu.roll(sum_y[c], LANES - EDGE, 1), 0.0)
            above = turned[c] if c < per_field - 1 else jnp.zeros_like(along_z)
            below = turned[c - 1] if c else jnp.zeros_like(along_z)
            along_x = jnp.where(upper, above, below)
            tag = tags[rows, c * LANES : (c + 1) * LANES].astype(jnp.float32)
            term = tag * (along_x + along_y + along_z)
            weight = term if c == 0 else weight + term
        weight_v[rows] = weight
        total = total + weight
    weight_v[pl.ds(tiles, 8)] = total

    src = lax.broadcasted_iota(jnp.int32, (LANES, LANES), 0)
    dst = lax.broadcasted_iota(jnp.int32, (LANES, LANES), 1)
    pick_y = ((src // EDGE) % EDGE == dst % EDGE).astype(jnp.float32)
    pick_z = (src % EDGE == dst).astype(jnp.float32)
    high = lax.Precision.HIGHEST
    by_y = jnp.dot(weight_v[:tiles], pick_y, precision=high, preferred_element_type=jnp.float32)
    by_z = jnp.dot(
        weight_v[pl.ds(tiles, 8)], pick_z, precision=high, preferred_element_type=jnp.float32
    )
    per_row = LANES // EDGE
    row_tile = lax.broadcasted_iota(jnp.int32, (per_row, LANES), 0)
    row_lane = lax.broadcasted_iota(jnp.int32, (per_row, LANES), 1)
    own = row_lane // EDGE == row_tile
    for r in range(y_rows):
        piece = jnp.where(own, by_y[r * per_row : (r + 1) * per_row], 0.0)
        line = 0.25 * jnp.sum(piece, axis=0, keepdims=True)
        for k in range(copies):
            parts[k, r] = line
    line = 0.25 * jnp.sum(by_z, axis=0, keepdims=True)
    for k in range(copies):
        parts[k, y_rows] = line
    for f in range(fields):
        for c in range(per_field):
            leave(f, c).wait()


def tile_step(got, coarse, tags, slabs):
    fields, tiles, cells = coarse.shape
    slot_rows = fields * cells // LANES
    blocks = got.shape[0] // (CAP * slot_rows + 1)
    part_rows = tiles * EDGE // LANES + 1
    vmem = pl.BlockSpec(memory_space=pltpu.VMEM)
    return pl.pallas_call(
        tile_kernel,
        out_shape=(
            jax.ShapeDtypeStruct(coarse.shape, jnp.float32),
            jax.ShapeDtypeStruct((slabs, part_rows, 1, LANES), jnp.float32),
        ),
        in_specs=[vmem, vmem, vmem],
        out_specs=(pl.BlockSpec(memory_space=pltpu.HBM), vmem),
        scratch_shapes=[
            pltpu.VMEM(((slot_rows + 1) * (tiles + 8), LANES), jnp.float32),
            pltpu.VMEM((1, LANES), jnp.int32),
            pltpu.SMEM((1, LANES), jnp.int32),
            pltpu.VMEM((tiles + 8, LANES), jnp.float32),
            pltpu.SemaphoreType.DMA((slot_rows + 1,)),
        ],
        compiler_params=pltpu.CompilerParams(vmem_limit_bytes=16 * 2**20),
        name="tile_step",
    )(got, coarse, tags)


def sum_kernel(along_y_cells, along_z_cells, parts, out):
    y_rows = parts.shape[1] - 1
    for r in range(y_rows + 1):
        line = parts[0, r]
        for k in range(1, parts.shape[0]):
            line = line + parts[k, r]
        if r < y_rows:
            out[:, r * LANES : (r + 1) * LANES] = line * (1.0 / along_y_cells)
        else:
            out[:, r * LANES :] = line[:, :EDGE] * (1.0 / along_z_cells)


def sum_parts(parts, tiles, slabs):
    width = tiles * EDGE + EDGE
    along_y_cells = EDGE * EDGE * slabs
    along_z_cells = EDGE * EDGE * tiles * slabs
    return pl.pallas_call(
        lambda p, o: sum_kernel(along_y_cells, along_z_cells, p, o),
        out_shape=jax.ShapeDtypeStruct((1, width), jnp.float32),
        in_specs=[pl.BlockSpec(memory_space=pltpu.VMEM)],
        out_specs=pl.BlockSpec(memory_space=pltpu.VMEM),
        name="sum_parts",
    )(parts)


def shards(coarse_fields, fine_fields, owner, target_tile, tags):
    tiles = coarse_fields.shape[0]
    blocks = lax.axis_size("blk")
    slabs = lax.axis_size("sig")
    sent = pack(owner[:, 0], target_tile[:, 0], fine_fields, blocks)
    got = lax.all_to_all(sent, "blk", split_axis=0, concat_axis=0, tiled=True)
    got = got.reshape(-1, LANES)
    coarse = jnp.transpose(coarse_fields, (1, 0, 2))
    synced, parts = tile_step(got, coarse, tags, slabs)
    parts = lax.all_to_all(parts, "sig", split_axis=0, concat_axis=0, tiled=True)
    signature = sum_parts(parts, tiles, slabs)
    return (jnp.transpose(synced, (1, 0, 2)), signature)


def solution(mesh):
    return jax.shard_map(
        shards,
        mesh=mesh,
        in_specs=(
            P(("blk", "sig"), None, None),
            P(("blk", "sig"), None, None, None),
            P(("blk", "sig"), None),
            P(("blk", "sig"), None),
            P(("blk", "sig"), None),
        ),
        out_specs=(P(("blk", "sig"), None, None), P("blk", None)),
        check_vma=False,
    )
```

```python
import functools

import jax
import jax.numpy as jnp
from jax import lax
from jax.experimental import pallas as pl
from jax.experimental.pallas import tpu as pltpu
from jax.sharding import PartitionSpec as P

EDGE = 8
CAP = 2
LANES = 128
CHUNKS = (3, 3, 1, 1)


def pack_kernel(owner, target, fine, out, buf, means, marks, owner_s, target_s, count, sems):
    patches, fields, children, cells = fine.shape
    chunk = patches // sum(CHUNKS)
    ends = [chunk * sum(CHUNKS[: k + 1]) for k in range(len(CHUNKS))]
    starts = [0] + ends[:-1]
    per_field = cells // LANES
    slot_rows = fields * per_field
    blocks = out.shape[0]

    def fetch(k):
        part = pl.ds(starts[k], ends[k] - starts[k])
        return pltpu.make_async_copy(fine.at[part], buf.at[part], sems.at[k])

    owner_copy = pltpu.make_async_copy(owner, owner_s, sems.at[len(CHUNKS)])
    target_copy = pltpu.make_async_copy(target, target_s, sems.at[len(CHUNKS) + 1])
    owner_copy.start()
    target_copy.start()
    for k in range(len(CHUNKS)):
        fetch(k).start()
    lane = lax.broadcasted_iota(jnp.int32, (1, LANES), 1)
    own_lane = CAP * lax.axis_index("blk")
    for o in range(blocks):
        count[o] = 0
        marks[o] = jnp.zeros((1, LANES), jnp.float32)
    owner_copy.wait()
    target_copy.wait()
    slots = []
    for i in range(patches):
        o = owner_s[i]
        rank = count[o]
        count[o] = rank + 1
        mark = (target_s[i] + 1).astype(jnp.float32)
        marks[o] = jnp.where(lane == own_lane + rank, mark, marks[o])
        slots.append((o, rank))
    leave_marks = pltpu.make_async_copy(marks, out.at[:, CAP * slot_rows], sems.at[len(CHUNKS) + 2])
    leave_marks.start()

    def leave(i):
        o, rank = slots[i]
        return pltpu.make_async_copy(
            means.at[pl.ds(i * slot_rows, slot_rows)],
            out.at[o, pl.ds(rank * slot_rows, slot_rows)],
            sems.at[len(CHUNKS) + 3 + i],
        )

    for k in range(len(CHUNKS)):
        fetch(k).wait()
        for i in range(starts[k], ends[k]):
            for f in range(fields):
                mean = 0.125 * jnp.sum(buf[i, f], axis=0, keepdims=True)
                for c in range(per_field):
                    means[i * slot_rows + f * per_field + c] = mean[:, c * LANES : (c + 1) * LANES]
            leave(i).start()
    leave_marks.wait()
    for i in range(patches):
        leave(i).wait()


def pack(owner, target, fine, blocks):
    patches, fields, children, cells = fine.shape
    slot_rows = fields * cells // LANES
    hbm = pl.BlockSpec(memory_space=pltpu.HBM)
    return pl.pallas_call(
        pack_kernel,
        out_shape=jax.ShapeDtypeStruct((blocks, CAP * slot_rows + 1, 1, LANES), jnp.float32),
        in_specs=[hbm, hbm, hbm],
        out_specs=hbm,
        scratch_shapes=[
            pltpu.VMEM(fine.shape, jnp.float32),
            pltpu.VMEM((patches * slot_rows, 1, LANES), jnp.float32),
            pltpu.VMEM((blocks, 1, LANES), jnp.float32),
            pltpu.SMEM((patches,), jnp.int32),
            pltpu.SMEM((patches,), jnp.int32),
            pltpu.SMEM((blocks,), jnp.int32),
            pltpu.SemaphoreType.DMA((len(CHUNKS) + 3 + patches,)),
        ],
        compiler_params=pltpu.CompilerParams(vmem_limit_bytes=64 * 2**20 - 2**17),
        name="pack_patches",
    )(owner, target, fine)


def tile_kernel(got, coarse, tags, fields_v, parts, weight_v):
    fields, tiles, cells = coarse.shape
    per_field = cells // LANES
    slot_rows = fields * per_field
    block = CAP * slot_rows + 1
    blocks = got.shape[0] // block
    pitch = tiles + 8
    copies, part_rows = parts.shape[0], parts.shape[1]
    y_rows = part_rows - 1

    marks = [None] * 4
    for b in range(blocks):
        row = got[pl.ds(b * block + CAP * slot_rows, 1)]
        marks[b % 4] = row if b < 4 else marks[b % 4] + row
    mark = ((marks[0] + marks[1]) + (marks[2] + marks[3])).astype(jnp.int32)
    tile_of = jnp.where(mark > 0, mark - 1, tiles)
    for f in range(fields):
        for c in range(per_field):
            fields_v[pl.ds((f * per_field + c) * pitch, tiles)] = coarse[
                f, :, c * LANES : (c + 1) * LANES
            ]
    for b in range(blocks):
        for r in range(CAP):
            tile = tile_of[0, CAP * b + r]
            base = b * block + r * slot_rows
            for j in range(0, slot_rows, 8):
                n = min(8, slot_rows - j)
                fields_v[pl.ds(tile + j * pitch, n, stride=pitch)] = got[base + j : base + j + n]

    lane = lax.broadcasted_iota(jnp.int32, (EDGE, LANES), 1)
    z = lane % EDGE
    y = (lane // EDGE) % EDGE
    upper = lane >= EDGE * EDGE
    inner_z = (z > 0) & (z < EDGE - 1)
    inner_y = (y > 0) & (y < EDGE - 1)
    total = jnp.zeros((EDGE, LANES), jnp.float32)
    for g in range(tiles // 8):
        rows = pl.ds(g * 8, 8)
        sum_z = [None] * per_field
        sum_y = [None] * per_field
        sum_x = [None] * (per_field - 1)
        for f in range(fields):
            v = [fields_v[pl.ds((f * per_field + c) * pitch + g * 8, 8)] for c in range(per_field)]
            for c in range(per_field):
                dz = v[c] - pltpu.roll(v[c], 2, 1)
                dy = v[c] - pltpu.roll(v[c], 2 * EDGE, 1)
                sum_z[c] = dz * dz if f == 0 else sum_z[c] + dz * dz
                sum_y[c] = dy * dy if f == 0 else sum_y[c] + dy * dy
                if c:
                    dx = v[c] - v[c - 1]
                    sum_x[c - 1] = dx * dx if f == 0 else sum_x[c - 1] + dx * dx
        turned = [pltpu.roll(s, EDGE * EDGE, 1) for s in sum_x]
        weight = None
        for c in range(per_field):
            along_z = jnp.where(inner_z, pltpu.roll(sum_z[c], LANES - 1, 1), 0.0)
            along_y = jnp.where(inner_y, pltpu.roll(sum_y[c], LANES - EDGE, 1), 0.0)
            above = turned[c] if c < per_field - 1 else jnp.zeros_like(along_z)
            below = turned[c - 1] if c else jnp.zeros_like(along_z)
            along_x = jnp.where(upper, above, below)
            tag = tags[rows, c * LANES : (c + 1) * LANES].astype(jnp.float32)
            term = tag * (along_x + along_y + along_z)
            weight = term if c == 0 else weight + term
        weight_v[rows] = weight
        total = total + weight
    weight_v[pl.ds(tiles, 8)] = total

    src = lax.broadcasted_iota(jnp.int32, (LANES, LANES), 0)
    dst = lax.broadcasted_iota(jnp.int32, (LANES, LANES), 1)
    pick_y = ((src // EDGE) % EDGE == dst % EDGE).astype(jnp.float32)
    pick_z = (src % EDGE == dst).astype(jnp.float32)
    high = lax.Precision.HIGHEST
    by_y = jnp.dot(weight_v[:tiles], pick_y, precision=high, preferred_element_type=jnp.float32)
    by_z = jnp.dot(
        weight_v[pl.ds(tiles, 8)], pick_z, precision=high, preferred_element_type=jnp.float32
    )
    per_row = LANES // EDGE
    row_tile = lax.broadcasted_iota(jnp.int32, (per_row, LANES), 0)
    row_lane = lax.broadcasted_iota(jnp.int32, (per_row, LANES), 1)
    own = row_lane // EDGE == row_tile
    for r in range(y_rows):
        piece = jnp.where(own, by_y[r * per_row : (r + 1) * per_row], 0.0)
        line = 0.25 * jnp.sum(piece, axis=0, keepdims=True)
        for k in range(copies):
            parts[k, r] = line
    line = 0.25 * jnp.sum(by_z, axis=0, keepdims=True)
    for k in range(copies):
        parts[k, y_rows] = line

def tile_step(got, coarse, tags, slabs):
    fields, tiles, cells = coarse.shape
    slot_rows = fields * cells // LANES
    blocks = got.shape[0] // (CAP * slot_rows + 1)
    part_rows = tiles * EDGE // LANES + 1
    vmem = pl.BlockSpec(memory_space=pltpu.VMEM)
    return pl.pallas_call(
        tile_kernel,
        out_shape=(
            jax.ShapeDtypeStruct(((slot_rows + 1) * (tiles + 8), LANES), jnp.float32),
            jax.ShapeDtypeStruct((slabs, part_rows, 1, LANES), jnp.float32),
        ),
        in_specs=[vmem, vmem, vmem],
        out_specs=(vmem, vmem),
        scratch_shapes=[
            pltpu.VMEM((tiles + 8, LANES), jnp.float32),
        ],
        compiler_params=pltpu.CompilerParams(vmem_limit_bytes=16 * 2**20),
        name="tile_step",
    )(got, coarse, tags)


def finish_kernel(along_y_cells, along_z_cells, fields_v, parts, synced, out, sems):
    fields, tiles, cells = synced.shape
    per_field = cells // LANES
    copies = [
        pltpu.make_async_copy(
            fields_v.at[pl.ds((f * per_field + c) * (tiles + 8), tiles)],
            synced.at[f, :, pl.ds(c * LANES, LANES)],
            sems.at[f * per_field + c],
        )
        for f in range(fields)
        for c in range(per_field)
    ]
    for copy in copies:
        copy.start()
    y_rows = parts.shape[1] - 1
    for r in range(y_rows + 1):
        line = parts[0, r]
        for k in range(1, parts.shape[0]):
            line = line + parts[k, r]
        if r < y_rows:
            out[:, r * LANES : (r + 1) * LANES] = line * (1.0 / along_y_cells)
        else:
            out[:, r * LANES :] = line[:, :EDGE] * (1.0 / along_z_cells)
    for copy in copies:
        copy.wait()


def finish(planes, parts, shape, slabs):
    fields, tiles, cells = shape
    width = tiles * EDGE + EDGE
    vmem = pl.BlockSpec(memory_space=pltpu.VMEM)
    return pl.pallas_call(
        functools.partial(finish_kernel, EDGE * EDGE * slabs, EDGE * EDGE * tiles * slabs),
        out_shape=(
            jax.ShapeDtypeStruct(shape, jnp.float32),
            jax.ShapeDtypeStruct((1, width), jnp.float32),
        ),
        in_specs=[vmem, vmem],
        out_specs=(pl.BlockSpec(memory_space=pltpu.HBM), vmem),
        scratch_shapes=[pltpu.SemaphoreType.DMA((fields * cells // LANES,))],
        compiler_params=pltpu.CompilerParams(vmem_limit_bytes=4 * 2**20),
        name="sum_and_write",
    )(planes, parts)


def shards(coarse_fields, fine_fields, owner, target_tile, tags):
    blocks = lax.axis_size("blk")
    slabs = lax.axis_size("sig")
    sent = pack(owner[:, 0], target_tile[:, 0], fine_fields, blocks)
    got = lax.all_to_all(sent, "blk", split_axis=0, concat_axis=0, tiled=True)
    got = got.reshape(-1, LANES)
    coarse = jnp.transpose(coarse_fields, (1, 0, 2))
    planes, parts = tile_step(got, coarse, tags, slabs)
    parts = lax.all_to_all(parts, "sig", split_axis=0, concat_axis=0, tiled=True)
    synced, signature = finish(planes, parts, coarse.shape, slabs)
    return (jnp.transpose(synced, (1, 0, 2)), signature)


def solution(mesh):
    return jax.shard_map(
        shards,
        mesh=mesh,
        in_specs=(
            P(("blk", "sig"), None, None),
            P(("blk", "sig"), None, None, None),
            P(("blk", "sig"), None),
            P(("blk", "sig"), None),
            P(("blk", "sig"), None),
        ),
        out_specs=(P(("blk", "sig"), None, None), P("blk", None)),
        check_vma=False,
    )
```

```python
import functools

import jax
import jax.numpy as jnp
from jax import lax
from jax.experimental import pallas as pl
from jax.experimental.pallas import tpu as pltpu
from jax.sharding import PartitionSpec as P

EDGE = 8
CAP = 2
LANES = 128
CHUNKS = (3, 3, 1, 1)


def pack_kernel(tiles, places, fine, out, buf, places_s, count, sems):
    patches, fields, children, cells = fine.shape
    chunk = patches // sum(CHUNKS)
    ends = [chunk * sum(CHUNKS[: k + 1]) for k in range(len(CHUNKS))]
    starts = [0] + ends[:-1]
    per_field = cells // LANES
    slot_rows = fields * per_field
    blocks = out.shape[0]

    def fetch(k):
        part = pl.ds(starts[k], ends[k] - starts[k])
        return pltpu.make_async_copy(fine.at[part], buf.at[part], sems.at[k])

    places_copy = pltpu.make_async_copy(places, places_s, sems.at[len(CHUNKS)])
    places_copy.start()
    for k in range(len(CHUNKS)):
        fetch(k).start()
    lane = lax.broadcasted_iota(jnp.int32, (1, LANES), 1)
    own_lane = CAP * lax.axis_index("blk")
    for o in range(blocks):
        count[o] = 0
        out[o, CAP * slot_rows] = jnp.zeros((1, LANES), jnp.float32)
    places_copy.wait()
    slots = []
    for i in range(patches):
        o = places_s[i] // tiles
        rank = count[o]
        count[o] = rank + 1
        mark = (places_s[i] - o * tiles + 1).astype(jnp.float32)
        row = CAP * slot_rows
        out[o, row] = jnp.where(lane == own_lane + rank, mark, out[o, row])
        slots.append((o, rank * slot_rows))
    for k in range(len(CHUNKS)):
        fetch(k).wait()
        for i in range(starts[k], ends[k]):
            o, row = slots[i]
            for f in range(fields):
                mean = 0.125 * jnp.sum(buf[i, f], axis=0, keepdims=True)
                for c in range(per_field):
                    out[o, row + f * per_field + c] = mean[:, c * LANES : (c + 1) * LANES]


def pack(places, fine, blocks, tiles):
    patches, fields, children, cells = fine.shape
    slot_rows = fields * cells // LANES
    hbm = pl.BlockSpec(memory_space=pltpu.HBM)
    return pl.pallas_call(
        functools.partial(pack_kernel, tiles),
        out_shape=jax.ShapeDtypeStruct((blocks, CAP * slot_rows + 1, 1, LANES), jnp.float32),
        in_specs=[pl.BlockSpec(memory_space=pl.ANY), hbm],
        out_specs=pl.BlockSpec(memory_space=pltpu.VMEM),
        scratch_shapes=[
            pltpu.VMEM(fine.shape, jnp.float32),
            pltpu.SMEM((patches,), jnp.int32),
            pltpu.SMEM((blocks,), jnp.int32),
            pltpu.SemaphoreType.DMA((len(CHUNKS) + 1,)),
        ],
        compiler_params=pltpu.CompilerParams(vmem_limit_bytes=int(52.5 * 2**20)),
        name="pack_patches",
    )(places, fine)


def tile_kernel(got, coarse, tags, fields_v, parts, weight_v):
    fields, tiles, cells = coarse.shape
    per_field = cells // LANES
    slot_rows = fields * per_field
    block = CAP * slot_rows + 1
    blocks = got.shape[0] // block
    pitch = tiles + 8
    copies, part_rows = parts.shape[0], parts.shape[1]
    y_rows = part_rows - 1

    marks = [None] * 4
    for b in range(blocks):
        row = got[pl.ds(b * block + CAP * slot_rows, 1)]
        marks[b % 4] = row if b < 4 else marks[b % 4] + row
    mark = ((marks[0] + marks[1]) + (marks[2] + marks[3])).astype(jnp.int32)
    tile_of = jnp.where(mark > 0, mark - 1, tiles)
    for f in range(fields):
        for c in range(per_field):
            fields_v[pl.ds((f * per_field + c) * pitch, tiles)] = coarse[
                f, :, c * LANES : (c + 1) * LANES
            ]
    for b in range(blocks):
        for r in range(CAP):
            tile = tile_of[0, CAP * b + r]
            base = b * block + r * slot_rows
            for j in range(0, slot_rows, 8):
                n = min(8, slot_rows - j)
                fields_v[pl.ds(tile + j * pitch, n, stride=pitch)] = got[base + j : base + j + n]

    lane = lax.broadcasted_iota(jnp.int32, (EDGE, LANES), 1)
    z = lane % EDGE
    y = (lane // EDGE) % EDGE
    upper = lane >= EDGE * EDGE
    inner_z = (z > 0) & (z < EDGE - 1)
    inner_y = (y > 0) & (y < EDGE - 1)
    total = jnp.zeros((EDGE, LANES), jnp.float32)
    for g in range(tiles // 8):
        rows = pl.ds(g * 8, 8)
        sum_z = [None] * per_field
        sum_y = [None] * per_field
        sum_x = [None] * (per_field - 1)
        for f in range(fields):
            v = [fields_v[pl.ds((f * per_field + c) * pitch + g * 8, 8)] for c in range(per_field)]
            for c in range(per_field):
                dz = v[c] - pltpu.roll(v[c], 2, 1)
                dy = v[c] - pltpu.roll(v[c], 2 * EDGE, 1)
                sum_z[c] = dz * dz if f == 0 else sum_z[c] + dz * dz
                sum_y[c] = dy * dy if f == 0 else sum_y[c] + dy * dy
                if c:
                    dx = v[c] - v[c - 1]
                    sum_x[c - 1] = dx * dx if f == 0 else sum_x[c - 1] + dx * dx
        turned = [pltpu.roll(s, EDGE * EDGE, 1) for s in sum_x]
        weight = None
        for c in range(per_field):
            along_z = jnp.where(inner_z, pltpu.roll(sum_z[c], LANES - 1, 1), 0.0)
            along_y = jnp.where(inner_y, pltpu.roll(sum_y[c], LANES - EDGE, 1), 0.0)
            above = turned[c] if c < per_field - 1 else jnp.zeros_like(along_z)
            below = turned[c - 1] if c else jnp.zeros_like(along_z)
            along_x = jnp.where(upper, above, below)
            tag = tags[rows, c * LANES : (c + 1) * LANES].astype(jnp.float32)
            term = tag * (along_x + along_y + along_z)
            weight = term if c == 0 else weight + term
        weight_v[rows] = weight
        total = total + weight
    weight_v[pl.ds(tiles, 8)] = total

    src = lax.broadcasted_iota(jnp.int32, (LANES, LANES), 0)
    dst = lax.broadcasted_iota(jnp.int32, (LANES, LANES), 1)
    pick_y = ((src // EDGE) % EDGE == dst % EDGE).astype(jnp.float32)
    pick_z = (src % EDGE == dst).astype(jnp.float32)
    high = lax.Precision.HIGHEST
    by_y = jnp.dot(weight_v[:tiles], pick_y, precision=high, preferred_element_type=jnp.float32)
    by_z = jnp.dot(
        weight_v[pl.ds(tiles, 8)], pick_z, precision=high, preferred_element_type=jnp.float32
    )
    per_row = LANES // EDGE
    row_tile = lax.broadcasted_iota(jnp.int32, (per_row, LANES), 0)
    row_lane = lax.broadcasted_iota(jnp.int32, (per_row, LANES), 1)
    own = row_lane // EDGE == row_tile
    for r in range(y_rows):
        piece = jnp.where(own, by_y[r * per_row : (r + 1) * per_row], 0.0)
        line = 0.25 * jnp.sum(piece, axis=0, keepdims=True)
        for k in range(copies):
            parts[k, r] = line
    line = 0.25 * jnp.sum(by_z, axis=0, keepdims=True)
    for k in range(copies):
        parts[k, y_rows] = line

def tile_step(got, coarse, tags, slabs):
    fields, tiles, cells = coarse.shape
    slot_rows = fields * cells // LANES
    blocks = got.shape[0] // (CAP * slot_rows + 1)
    part_rows = tiles * EDGE // LANES + 1
    vmem = pl.BlockSpec(memory_space=pltpu.VMEM)
    return pl.pallas_call(
        tile_kernel,
        out_shape=(
            jax.ShapeDtypeStruct(((slot_rows + 1) * (tiles + 8), LANES), jnp.float32),
            jax.ShapeDtypeStruct((slabs, part_rows, 1, LANES), jnp.float32),
        ),
        in_specs=[vmem, vmem, vmem],
        out_specs=(vmem, vmem),
        scratch_shapes=[
            pltpu.VMEM((tiles + 8, LANES), jnp.float32),
        ],
        compiler_params=pltpu.CompilerParams(vmem_limit_bytes=16 * 2**20),
        name="tile_step",
    )(got, coarse, tags)


def finish_kernel(along_y_cells, along_z_cells, fields_v, parts, synced, signature, out, sems):
    fields, tiles, cells = synced.shape
    per_field = cells // LANES
    copies = [
        pltpu.make_async_copy(
            fields_v.at[pl.ds((f * per_field + c) * (tiles + 8), tiles)],
            synced.at[f, :, pl.ds(c * LANES, LANES)],
            sems.at[f * per_field + c],
        )
        for f in range(fields)
        for c in range(per_field)
    ]
    for copy in copies:
        copy.start()
    y_rows = parts.shape[1] - 1
    for r in range(y_rows + 1):
        line = parts[0, r]
        for k in range(1, parts.shape[0]):
            line = line + parts[k, r]
        if r < y_rows:
            out[:, r * LANES : (r + 1) * LANES] = line * (1.0 / along_y_cells)
        else:
            out[:, r * LANES :] = line[:, :EDGE] * (1.0 / along_z_cells)
    last = pltpu.make_async_copy(out, signature, sems.at[len(copies)])
    last.start()
    for copy in copies:
        copy.wait()
    last.wait()


def finish(planes, parts, shape, slabs):
    fields, tiles, cells = shape
    width = tiles * EDGE + EDGE
    vmem = pl.BlockSpec(memory_space=pltpu.VMEM)
    hbm = pl.BlockSpec(memory_space=pltpu.HBM)
    return pl.pallas_call(
        functools.partial(finish_kernel, EDGE * EDGE * slabs, EDGE * EDGE * tiles * slabs),
        out_shape=(
            jax.ShapeDtypeStruct(shape, jnp.float32),
            jax.ShapeDtypeStruct((1, width), jnp.float32),
        ),
        in_specs=[vmem, vmem],
        out_specs=(hbm, hbm),
        scratch_shapes=[
            pltpu.VMEM((1, width), jnp.float32),
            pltpu.SemaphoreType.DMA((fields * cells // LANES + 1,)),
        ],
        compiler_params=pltpu.CompilerParams(vmem_limit_bytes=4 * 2**20),
        name="sum_and_write",
    )(planes, parts)


def shards(coarse_fields, fine_fields, owner, target_tile, tags):
    blocks = lax.axis_size("blk")
    slabs = lax.axis_size("sig")
    tiles = coarse_fields.shape[0]
    places = owner[:, 0] * tiles + target_tile[:, 0]
    sent = pack(places, fine_fields, blocks, tiles)
    got = lax.all_to_all(sent, "blk", split_axis=0, concat_axis=0, tiled=True)
    got = got.reshape(-1, LANES)
    coarse = jnp.transpose(coarse_fields, (1, 0, 2))
    planes, parts = tile_step(got, coarse, tags, slabs)
    parts = lax.all_to_all(parts, "sig", split_axis=0, concat_axis=0, tiled=True)
    synced, signature = finish(planes, parts, coarse.shape, slabs)
    return (jnp.transpose(synced, (1, 0, 2)), signature)


def solution(mesh):
    return jax.shard_map(
        shards,
        mesh=mesh,
        in_specs=(
            P(("blk", "sig"), None, None),
            P(("blk", "sig"), None, None, None),
            P(("blk", "sig"), None),
            P(("blk", "sig"), None),
            P(("blk", "sig"), None),
        ),
        out_specs=(P(("blk", "sig"), None, None), P("blk", None)),
        check_vma=False,
    )
```

```python
import functools

import jax
import jax.numpy as jnp
from jax import lax
from jax.experimental import pallas as pl
from jax.experimental.pallas import tpu as pltpu
from jax.sharding import PartitionSpec as P

EDGE = 8
CAP = 2
LANES = 128
CHUNKS = (3, 3, 1, 1)


def pack_kernel(tiles, places, fine, out, buf, places_s, count, sems):
    patches, fields, children, cells = fine.shape
    chunk = patches // sum(CHUNKS)
    ends = [chunk * sum(CHUNKS[: k + 1]) for k in range(len(CHUNKS))]
    starts = [0] + ends[:-1]
    per_field = cells // LANES
    slot_rows = fields * per_field
    blocks = out.shape[0]

    def fetch(k):
        part = pl.ds(starts[k], ends[k] - starts[k])
        return pltpu.make_async_copy(fine.at[part], buf.at[part], sems.at[k])

    places_copy = pltpu.make_async_copy(places, places_s, sems.at[len(CHUNKS)])
    places_copy.start()
    for k in range(len(CHUNKS)):
        fetch(k).start()
    lane = lax.broadcasted_iota(jnp.int32, (1, LANES), 1)
    own_lane = CAP * lax.axis_index("blk")
    for o in range(blocks):
        count[o] = 0
        out[o, CAP * slot_rows] = jnp.zeros((1, LANES), jnp.float32)
    places_copy.wait()
    slots = []
    for i in range(patches):
        o = places_s[i] // tiles
        rank = count[o]
        count[o] = rank + 1
        mark = (places_s[i] - o * tiles + 1).astype(jnp.float32)
        row = CAP * slot_rows
        out[o, row] = jnp.where(lane == own_lane + rank, mark, out[o, row])
        slots.append((o, rank * slot_rows))
    for k in range(len(CHUNKS)):
        fetch(k).wait()
        for i in range(starts[k], ends[k]):
            o, row = slots[i]
            for f in range(fields):
                mean = 0.125 * jnp.sum(buf[i, f], axis=0, keepdims=True)
                for c in range(per_field):
                    out[o, row + f * per_field + c] = mean[:, c * LANES : (c + 1) * LANES]


def pack(places, fine, blocks, tiles):
    patches, fields, children, cells = fine.shape
    slot_rows = fields * cells // LANES
    hbm = pl.BlockSpec(memory_space=pltpu.HBM)
    return pl.pallas_call(
        functools.partial(pack_kernel, tiles),
        out_shape=jax.ShapeDtypeStruct((blocks, CAP * slot_rows + 1, 1, LANES), jnp.float32),
        in_specs=[pl.BlockSpec(memory_space=pl.ANY), hbm],
        out_specs=pl.BlockSpec(memory_space=pltpu.VMEM),
        scratch_shapes=[
            pltpu.VMEM(fine.shape, jnp.float32),
            pltpu.SMEM((patches,), jnp.int32),
            pltpu.SMEM((blocks,), jnp.int32),
            pltpu.SemaphoreType.DMA((len(CHUNKS) + 1,)),
        ],
        compiler_params=pltpu.CompilerParams(vmem_limit_bytes=int(52.5 * 2**20)),
        name="pack_patches",
    )(places, fine)


def tile_kernel(got, coarse, tags, fields_v, parts, weight_v, ahead_v):
    fields, tiles, cells = coarse.shape
    per_field = cells // LANES
    slot_rows = fields * per_field
    block = CAP * slot_rows + 1
    blocks = got.shape[0] // block
    pitch = tiles + 8
    copies, part_rows = parts.shape[0], parts.shape[1]
    y_rows = part_rows - 1

    marks = [None] * 4
    for b in range(blocks):
        row = got[pl.ds(b * block + CAP * slot_rows, 1)]
        marks[b % 4] = row if b < 4 else marks[b % 4] + row
    mark = ((marks[0] + marks[1]) + (marks[2] + marks[3])).astype(jnp.int32)
    tile_of = jnp.where(mark > 0, mark - 1, tiles)
    for f in range(fields):
        for c in range(per_field):
            fields_v[pl.ds((f * per_field + c) * pitch, tiles)] = coarse[
                f, :, c * LANES : (c + 1) * LANES
            ]
    for b in range(blocks):
        for r in range(CAP):
            tile = tile_of[0, CAP * b + r]
            base = b * block + r * slot_rows
            for j in range(0, slot_rows, 8):
                n = min(8, slot_rows - j)
                fields_v[pl.ds(tile + j * pitch, n, stride=pitch)] = got[base + j : base + j + n]

    lane = lax.broadcasted_iota(jnp.int32, (EDGE, LANES), 1)
    z = lane % EDGE
    y = (lane // EDGE) % EDGE
    upper = lane >= EDGE * EDGE
    for g in range(tiles // 8):
        rows = pl.ds(g * 8, 8)
        sum_z = [None] * per_field
        sum_y = [None] * per_field
        sum_x = [None] * (per_field - 1)
        for f in range(fields):
            v = [fields_v[pl.ds((f * per_field + c) * pitch + g * 8, 8)] for c in range(per_field)]
            for c in range(per_field):
                dz = v[c] - pltpu.roll(v[c], 2, 1)
                dy = v[c] - pltpu.roll(v[c], 2 * EDGE, 1)
                sum_z[c] = dz * dz if f == 0 else sum_z[c] + dz * dz
                sum_y[c] = dy * dy if f == 0 else sum_y[c] + dy * dy
                if c:
                    dx = v[c] - v[c - 1]
                    sum_x[c - 1] = dx * dx if f == 0 else sum_x[c - 1] + dx * dx
        tag = [tags[rows, c * LANES : (c + 1) * LANES].astype(jnp.float32) for c in range(per_field)]
        half = [pltpu.roll(s, EDGE * EDGE, 1) for s in tag]
        by_x = by_y = by_z = None
        for c in range(per_field):
            tag_y = jnp.where(y >= 2, pltpu.roll(tag[c], EDGE, 1), 0.0)
            tag_z = jnp.where(z >= 2, pltpu.roll(tag[c], 1, 1), 0.0)
            by_y = tag_y * sum_y[c] if c == 0 else by_y + tag_y * sum_y[c]
            by_z = tag_z * sum_z[c] if c == 0 else by_z + tag_z * sum_z[c]
            if c:
                term = jnp.where(upper, half[c], half[c - 1]) * sum_x[c - 1]
                by_x = term if c == 1 else by_x + term
        weight_v[rows] = by_x
        ahead_v[0, rows] = by_y
        ahead_v[1, rows] = by_z
    total = None
    for g in range(tiles // 8):
        rows = pl.ds(g * 8, 8)
        weight = (
            weight_v[rows]
            + pltpu.roll(ahead_v[0, rows], LANES - EDGE, 1)
            + pltpu.roll(ahead_v[1, rows], LANES - 1, 1)
        )
        weight_v[rows] = weight
        total = weight if g == 0 else total + weight
    weight_v[pl.ds(tiles, 8)] = total

    src = lax.broadcasted_iota(jnp.int32, (LANES, LANES), 0)
    dst = lax.broadcasted_iota(jnp.int32, (LANES, LANES), 1)
    pick_y = ((src // EDGE) % EDGE == dst % EDGE).astype(jnp.float32)
    pick_z = (src % EDGE == dst).astype(jnp.float32)
    high = lax.Precision.HIGHEST
    by_y = jnp.dot(weight_v[:tiles], pick_y, precision=high, preferred_element_type=jnp.float32)
    by_z = jnp.dot(
        weight_v[pl.ds(tiles, 8)], pick_z, precision=high, preferred_element_type=jnp.float32
    )
    per_row = LANES // EDGE
    row_tile = lax.broadcasted_iota(jnp.int32, (per_row, LANES), 0)
    row_lane = lax.broadcasted_iota(jnp.int32, (per_row, LANES), 1)
    own = row_lane // EDGE == row_tile
    for r in range(y_rows):
        piece = jnp.where(own, by_y[r * per_row : (r + 1) * per_row], 0.0)
        line = 0.25 * jnp.sum(piece, axis=0, keepdims=True)
        for k in range(copies):
            parts[k, r] = line
    line = 0.25 * jnp.sum(by_z, axis=0, keepdims=True)
    for k in range(copies):
        parts[k, y_rows] = line

def tile_step(got, coarse, tags, slabs):
    fields, tiles, cells = coarse.shape
    slot_rows = fields * cells // LANES
    blocks = got.shape[0] // (CAP * slot_rows + 1)
    part_rows = tiles * EDGE // LANES + 1
    vmem = pl.BlockSpec(memory_space=pltpu.VMEM)
    return pl.pallas_call(
        tile_kernel,
        out_shape=(
            jax.ShapeDtypeStruct(((slot_rows + 1) * (tiles + 8), LANES), jnp.float32),
            jax.ShapeDtypeStruct((slabs, part_rows, 1, LANES), jnp.float32),
        ),
        in_specs=[vmem, vmem, vmem],
        out_specs=(vmem, vmem),
        scratch_shapes=[
            pltpu.VMEM((tiles + 8, LANES), jnp.float32),
            pltpu.VMEM((2, tiles, LANES), jnp.float32),
        ],
        compiler_params=pltpu.CompilerParams(vmem_limit_bytes=16 * 2**20),
        name="tile_step",
    )(got, coarse, tags)


def finish_kernel(along_y_cells, along_z_cells, fields_v, parts, synced, signature, out, sems):
    fields, tiles, cells = synced.shape
    per_field = cells // LANES
    copies = [
        pltpu.make_async_copy(
            fields_v.at[pl.ds((f * per_field + c) * (tiles + 8), tiles)],
            synced.at[f, :, pl.ds(c * LANES, LANES)],
            sems.at[f * per_field + c],
        )
        for f in range(fields)
        for c in range(per_field)
    ]
    for copy in copies:
        copy.start()
    y_rows = parts.shape[1] - 1
    for r in range(y_rows + 1):
        line = parts[0, r]
        for k in range(1, parts.shape[0]):
            line = line + parts[k, r]
        if r < y_rows:
            out[:, r * LANES : (r + 1) * LANES] = line * (1.0 / along_y_cells)
        else:
            out[:, r * LANES :] = line[:, :EDGE] * (1.0 / along_z_cells)
    last = pltpu.make_async_copy(out, signature, sems.at[len(copies)])
    last.start()
    for copy in copies:
        copy.wait()
    last.wait()


def finish(planes, parts, shape, slabs):
    fields, tiles, cells = shape
    width = tiles * EDGE + EDGE
    vmem = pl.BlockSpec(memory_space=pltpu.VMEM)
    hbm = pl.BlockSpec(memory_space=pltpu.HBM)
    return pl.pallas_call(
        functools.partial(finish_kernel, EDGE * EDGE * slabs, EDGE * EDGE * tiles * slabs),
        out_shape=(
            jax.ShapeDtypeStruct(shape, jnp.float32),
            jax.ShapeDtypeStruct((1, width), jnp.float32),
        ),
        in_specs=[vmem, vmem],
        out_specs=(hbm, hbm),
        scratch_shapes=[
            pltpu.VMEM((1, width), jnp.float32),
            pltpu.SemaphoreType.DMA((fields * cells // LANES + 1,)),
        ],
        compiler_params=pltpu.CompilerParams(vmem_limit_bytes=4 * 2**20),
        name="sum_and_write",
    )(planes, parts)


def shards(coarse_fields, fine_fields, owner, target_tile, tags):
    blocks = lax.axis_size("blk")
    slabs = lax.axis_size("sig")
    tiles = coarse_fields.shape[0]
    places = owner[:, 0] * tiles + target_tile[:, 0]
    sent = pack(places, fine_fields, blocks, tiles)
    got = lax.all_to_all(sent, "blk", split_axis=0, concat_axis=0, tiled=True)
    got = got.reshape(-1, LANES)
    coarse = jnp.transpose(coarse_fields, (1, 0, 2))
    planes, parts = tile_step(got, coarse, tags, slabs)
    parts = lax.all_to_all(parts, "sig", split_axis=0, concat_axis=0, tiled=True)
    synced, signature = finish(planes, parts, coarse.shape, slabs)
    return (jnp.transpose(synced, (1, 0, 2)), signature)


def solution(mesh):
    return jax.shard_map(
        shards,
        mesh=mesh,
        in_specs=(
            P(("blk", "sig"), None, None),
            P(("blk", "sig"), None, None, None),
            P(("blk", "sig"), None),
            P(("blk", "sig"), None),
            P(("blk", "sig"), None),
        ),
        out_specs=(P(("blk", "sig"), None, None), P("blk", None)),
        check_vma=False,
    )
```

```python
import functools

import jax
import jax.numpy as jnp
from jax import lax
from jax.experimental import pallas as pl
from jax.experimental.pallas import tpu as pltpu
from jax.sharding import PartitionSpec as P

EDGE = 8
CAP = 2
LANES = 128
CHUNKS = (3, 3, 1, 1)


def pack_kernel(tiles, places, fine, out, buf, places_s, count, sems):
    patches, fields, children, cells = fine.shape
    chunk = patches // sum(CHUNKS)
    ends = [chunk * sum(CHUNKS[: k + 1]) for k in range(len(CHUNKS))]
    starts = [0] + ends[:-1]
    per_field = cells // LANES
    slot_rows = fields * per_field
    blocks = out.shape[0]

    def fetch(k):
        part = pl.ds(starts[k], ends[k] - starts[k])
        return pltpu.make_async_copy(fine.at[part], buf.at[part], sems.at[k])

    places_copy = pltpu.make_async_copy(places, places_s, sems.at[len(CHUNKS)])
    places_copy.start()
    for k in range(len(CHUNKS)):
        fetch(k).start()
    lane = lax.broadcasted_iota(jnp.int32, (1, LANES), 1)
    own_lane = CAP * lax.axis_index("blk")
    for o in range(blocks):
        count[o] = 0
        out[o, CAP * slot_rows] = jnp.zeros((1, LANES), jnp.float32)
    places_copy.wait()
    slots = []
    for i in range(patches):
        o = places_s[i] // tiles
        rank = count[o]
        count[o] = rank + 1
        mark = (places_s[i] - o * tiles + 1).astype(jnp.float32)
        row = CAP * slot_rows
        out[o, row] = jnp.where(lane == own_lane + rank, mark, out[o, row])
        slots.append((o, rank * slot_rows))
    for k in range(len(CHUNKS)):
        fetch(k).wait()
        for i in range(starts[k], ends[k]):
            o, row = slots[i]
            for f in range(fields):
                mean = 0.125 * jnp.sum(buf[i, f], axis=0, keepdims=True)
                for c in range(per_field):
                    out[o, row + f * per_field + c] = mean[:, c * LANES : (c + 1) * LANES]


def pack(places, fine, blocks, tiles):
    patches, fields, children, cells = fine.shape
    slot_rows = fields * cells // LANES
    hbm = pl.BlockSpec(memory_space=pltpu.HBM)
    return pl.pallas_call(
        functools.partial(pack_kernel, tiles),
        out_shape=jax.ShapeDtypeStruct((blocks, CAP * slot_rows + 1, 1, LANES), jnp.float32),
        in_specs=[pl.BlockSpec(memory_space=pl.ANY), hbm],
        out_specs=pl.BlockSpec(memory_space=pltpu.VMEM),
        scratch_shapes=[
            pltpu.VMEM(fine.shape, jnp.float32),
            pltpu.SMEM((patches,), jnp.int32),
            pltpu.SMEM((blocks,), jnp.int32),
            pltpu.SemaphoreType.DMA((len(CHUNKS) + 1,)),
        ],
        compiler_params=pltpu.CompilerParams(vmem_limit_bytes=int(52.5 * 2**20)),
        name="pack_patches",
    )(places, fine)


def tile_kernel(got, coarse, tags, merged, parts, fields_v, weight_v, ahead_v):
    fields, tiles, cells = coarse.shape
    per_field = cells // LANES
    slot_rows = fields * per_field
    block = CAP * slot_rows + 1
    blocks = got.shape[0] // block
    pitch = tiles + 8
    copies, part_rows = parts.shape[0], parts.shape[1]
    y_rows = part_rows - 1

    marks = [None] * 4
    for b in range(blocks):
        row = got[pl.ds(b * block + CAP * slot_rows, 1)]
        marks[b % 4] = row if b < 4 else marks[b % 4] + row
    mark = ((marks[0] + marks[1]) + (marks[2] + marks[3])).astype(jnp.int32)
    tile_of = jnp.where(mark > 0, mark - 1, tiles)
    for f in range(fields):
        for c in range(per_field):
            fields_v[pl.ds((f * per_field + c) * pitch, tiles)] = coarse[
                f, :, c * LANES : (c + 1) * LANES
            ]
    for b in range(blocks):
        for r in range(CAP):
            tile = tile_of[0, CAP * b + r]
            base = b * block + r * slot_rows
            for j in range(0, slot_rows, 8):
                n = min(8, slot_rows - j)
                fields_v[pl.ds(tile + j * pitch, n, stride=pitch)] = got[base + j : base + j + n]

    lane = lax.broadcasted_iota(jnp.int32, (EDGE, LANES), 1)
    z = lane % EDGE
    y = (lane // EDGE) % EDGE
    upper = lane >= EDGE * EDGE
    for g in range(tiles // 8):
        rows = pl.ds(g * 8, 8)
        sum_z = [None] * per_field
        sum_y = [None] * per_field
        sum_x = [None] * (per_field - 1)
        for f in range(fields):
            v = [fields_v[pl.ds((f * per_field + c) * pitch + g * 8, 8)] for c in range(per_field)]
            for c in range(per_field):
                merged[f, rows, c * LANES : (c + 1) * LANES] = v[c]
                dz = v[c] - pltpu.roll(v[c], 2, 1)
                dy = v[c] - pltpu.roll(v[c], 2 * EDGE, 1)
                sum_z[c] = dz * dz if f == 0 else sum_z[c] + dz * dz
                sum_y[c] = dy * dy if f == 0 else sum_y[c] + dy * dy
                if c:
                    dx = v[c] - v[c - 1]
                    sum_x[c - 1] = dx * dx if f == 0 else sum_x[c - 1] + dx * dx
        tag = [tags[rows, c * LANES : (c + 1) * LANES].astype(jnp.float32) for c in range(per_field)]
        half = [pltpu.roll(s, EDGE * EDGE, 1) for s in tag]
        by_x = by_y = by_z = None
        for c in range(per_field):
            tag_y = jnp.where(y >= 2, pltpu.roll(tag[c], EDGE, 1), 0.0)
            tag_z = jnp.where(z >= 2, pltpu.roll(tag[c], 1, 1), 0.0)
            by_y = tag_y * sum_y[c] if c == 0 else by_y + tag_y * sum_y[c]
            by_z = tag_z * sum_z[c] if c == 0 else by_z + tag_z * sum_z[c]
            if c:
                term = jnp.where(upper, half[c], half[c - 1]) * sum_x[c - 1]
                by_x = term if c == 1 else by_x + term
        weight_v[rows] = by_x
        ahead_v[0, rows] = by_y
        ahead_v[1, rows] = by_z
    total = None
    for g in range(tiles // 8):
        rows = pl.ds(g * 8, 8)
        weight = (
            weight_v[rows]
            + pltpu.roll(ahead_v[0, rows], LANES - EDGE, 1)
            + pltpu.roll(ahead_v[1, rows], LANES - 1, 1)
        )
        weight_v[rows] = weight
        total = weight if g == 0 else total + weight
    weight_v[pl.ds(tiles, 8)] = total

    src = lax.broadcasted_iota(jnp.int32, (LANES, LANES), 0)
    dst = lax.broadcasted_iota(jnp.int32, (LANES, LANES), 1)
    pick_y = ((src // EDGE) % EDGE == dst % EDGE).astype(jnp.float32)
    pick_z = (src % EDGE == dst).astype(jnp.float32)
    high = lax.Precision.HIGHEST
    by_y = jnp.dot(weight_v[:tiles], pick_y, precision=high, preferred_element_type=jnp.float32)
    by_z = jnp.dot(
        weight_v[pl.ds(tiles, 8)], pick_z, precision=high, preferred_element_type=jnp.float32
    )
    per_row = LANES // EDGE
    row_tile = lax.broadcasted_iota(jnp.int32, (per_row, LANES), 0)
    row_lane = lax.broadcasted_iota(jnp.int32, (per_row, LANES), 1)
    own = row_lane // EDGE == row_tile
    for r in range(y_rows):
        piece = jnp.where(own, by_y[r * per_row : (r + 1) * per_row], 0.0)
        line = 0.25 * jnp.sum(piece, axis=0, keepdims=True)
        for k in range(copies):
            parts[k, r] = line
    line = 0.25 * jnp.sum(by_z, axis=0, keepdims=True)
    for k in range(copies):
        parts[k, y_rows] = line

def tile_step(got, coarse, tags, slabs):
    fields, tiles, cells = coarse.shape
    slot_rows = fields * cells // LANES
    blocks = got.shape[0] // (CAP * slot_rows + 1)
    part_rows = tiles * EDGE // LANES + 1
    vmem = pl.BlockSpec(memory_space=pltpu.VMEM)
    return pl.pallas_call(
        tile_kernel,
        out_shape=(
            jax.ShapeDtypeStruct(coarse.shape, jnp.float32),
            jax.ShapeDtypeStruct((slabs, part_rows, 1, LANES), jnp.float32),
        ),
        in_specs=[vmem, vmem, vmem],
        out_specs=(vmem, vmem),
        scratch_shapes=[
            pltpu.VMEM(((slot_rows + 1) * (tiles + 8), LANES), jnp.float32),
            pltpu.VMEM((tiles + 8, LANES), jnp.float32),
            pltpu.VMEM((2, tiles, LANES), jnp.float32),
        ],
        compiler_params=pltpu.CompilerParams(vmem_limit_bytes=16 * 2**20),
        name="tile_step",
    )(got, coarse, tags)


def finish_kernel(along_y_cells, along_z_cells, merged, parts, synced, signature, out, sems):
    tiles_copy = pltpu.make_async_copy(merged, synced, sems.at[0])
    tiles_copy.start()
    y_rows = parts.shape[1] - 1
    for r in range(y_rows + 1):
        line = parts[0, r]
        for k in range(1, parts.shape[0]):
            line = line + parts[k, r]
        if r < y_rows:
            out[:, r * LANES : (r + 1) * LANES] = line * (1.0 / along_y_cells)
        else:
            out[:, r * LANES :] = line[:, :EDGE] * (1.0 / along_z_cells)
    last = pltpu.make_async_copy(out, signature, sems.at[1])
    last.start()
    tiles_copy.wait()
    last.wait()


def finish(merged, parts, slabs):
    tiles = merged.shape[1]
    width = tiles * EDGE + EDGE
    vmem = pl.BlockSpec(memory_space=pltpu.VMEM)
    hbm = pl.BlockSpec(memory_space=pltpu.HBM)
    return pl.pallas_call(
        functools.partial(finish_kernel, EDGE * EDGE * slabs, EDGE * EDGE * tiles * slabs),
        out_shape=(
            jax.ShapeDtypeStruct(merged.shape, jnp.float32),
            jax.ShapeDtypeStruct((1, width), jnp.float32),
        ),
        in_specs=[vmem, vmem],
        out_specs=(hbm, hbm),
        scratch_shapes=[
            pltpu.VMEM((1, width), jnp.float32),
            pltpu.SemaphoreType.DMA((2,)),
        ],
        compiler_params=pltpu.CompilerParams(vmem_limit_bytes=4 * 2**20),
        name="sum_and_write",
    )(merged, parts)


def shards(coarse_fields, fine_fields, owner, target_tile, tags):
    blocks = lax.axis_size("blk")
    slabs = lax.axis_size("sig")
    tiles = coarse_fields.shape[0]
    places = owner[:, 0] * tiles + target_tile[:, 0]
    sent = pack(places, fine_fields, blocks, tiles)
    got = lax.all_to_all(sent, "blk", split_axis=0, concat_axis=0, tiled=True)
    got = got.reshape(-1, LANES)
    coarse = jnp.transpose(coarse_fields, (1, 0, 2))
    merged, parts = tile_step(got, coarse, tags, slabs)
    parts = lax.all_to_all(parts, "sig", split_axis=0, concat_axis=0, tiled=True)
    synced, signature = finish(merged, parts, slabs)
    return (jnp.transpose(synced, (1, 0, 2)), signature)


def solution(mesh):
    return jax.shard_map(
        shards,
        mesh=mesh,
        in_specs=(
            P(("blk", "sig"), None, None),
            P(("blk", "sig"), None, None, None),
            P(("blk", "sig"), None),
            P(("blk", "sig"), None),
            P(("blk", "sig"), None),
        ),
        out_specs=(P(("blk", "sig"), None, None), P("blk", None)),
        check_vma=False,
    )
```
